32 devices in a mesh: dp: 4 (over z), clus: 8 (over y, x, core).
Axes of the slice: x: 2, y: 2, z: 4, core: 2. Of those that a mesh axis runs over, the one named last changes fastest.
Arguments:
- points: bfloat16 [128, 128, 1024], P(('dp', 'clus')), may hold values from -40 to 40
- block_cluster: int32 [128, 1], P(('dp', 'clus')), may hold values from 0 to 63, as said below
- queries: bfloat16 [512, 1024], P(('dp', 'clus')), may hold values from -6 to 6
- query_ids: int32 [64, 128], P(('dp', 'clus')), may hold values from 0 to 511
Outputs:
- gram_tiles: float32 [64, 1024, 1024], P(('dp', 'clus'))
- cross: float32 [64, 1024, 128], P(('dp', 'clus'))
The draws below stay inside these ranges and needn't reach their ends.
Inputs may be any that keep to these rules, and one draw needn't show every extreme that they name: `block_cluster`: cluster c is owned by the device at position c // 2 in the order of dp+clus, dp slowest. Of the 4 blocks of one device, at most 2 belong to clusters whose owners share one index along clus, exactly 2 for some device and index. Of all blocks on the devices of one index along dp, those whose owners share one index along clus number at most 3 for each owner index along dp, exactly 3 for some.
All inputs are finite; a program needn't handle non-finite values.
Results may differ from the reference program's by a relative error of at most 0.0022.
Values may be sent and summed in bfloat16 or wider, within the bound.
No kernel may reach another device: no remote copies, remote signals or barrier semaphores. Data moves between devices by JAX's collectives and lax.ppermute only.
A program may use at most 128 MiB of HBM per device.

```python
import math
import jax
import jax.numpy as jnp
from jax import lax

D = 1024
BLK = 128
CL_OWN = 2
MQ = 128
CLUSTERS = 64
NB = 4
BLOCKS = 128
NQ = 512
MEANROWS = 256
CB = 3
N_DP = 4
N_CLUS = 8


def draw_points(key, part):
    keys = jax.random.split(jax.random.fold_in(key, 5), 3)
    row_scale = jnp.exp(jax.random.uniform(keys[0], (BLOCKS, BLK, 1), jnp.float32, math.log(0.25), math.log(2.5)))
    col_scale = jnp.exp(jax.random.uniform(keys[1], (1, 1, D), jnp.float32, math.log(0.4), math.log(4.0)))
    base = jnp.clip(jax.random.normal(keys[2], (BLOCKS, BLK, D), jnp.float32), -4.0, 4.0)
    return (base * row_scale * col_scale).astype(jnp.bfloat16)


def draw_row_routes(row_key):
    full_cap = N_DP * CB
    others = N_CLUS - 1
    keys = jax.random.split(row_key, 7)
    col_order = jax.random.permutation(keys[0], N_CLUS).astype(jnp.int32)
    slot_count = others * full_cap
    slot_index = jnp.arange(slot_count, dtype=jnp.int32)
    slot_col = slot_index // full_cap
    col_weight = jax.random.randint(keys[1], (others,), 1, 5).astype(jnp.int32)
    noise = jax.random.randint(keys[2], (slot_count,), 0, 1024).astype(jnp.int32)
    priority = noise * col_weight[slot_col] * slot_count + slot_index
    chosen_order = jnp.argsort(priority, stable=True)
    remaining = N_CLUS * NB - full_cap
    chosen = jnp.zeros((slot_count,), jnp.int32).at[chosen_order[:remaining]].set(1)
    counts_other = jnp.sum(chosen.reshape(others, full_cap), axis=1)
    counts = jnp.concatenate([jnp.full((1,), full_cap, jnp.int32), counts_other.astype(jnp.int32)])
    ends = jnp.cumsum(counts).astype(jnp.int32)
    starts = ends - counts
    token = jnp.arange(N_CLUS * NB, dtype=jnp.int32)
    token_col = jnp.sum((token[:, None] >= ends[None, :]).astype(jnp.int32), axis=1)
    rank_in_col = token - starts[token_col]
    perm_keys = jax.random.split(keys[3], N_CLUS)
    perms = jax.vmap(lambda one_key: jax.random.permutation(one_key, full_cap))(perm_keys).astype(jnp.int32)
    target_dp = perms[token_col, rank_in_col] // CB
    local = jax.random.randint(keys[4], (N_CLUS * NB,), 0, CL_OWN).astype(jnp.int32)
    cluster = (target_dp * N_CLUS + col_order[token_col]) * CL_OWN + local
    by_position = cluster.reshape(NB, N_CLUS).T
    shuffle_keys = jax.random.split(keys[5], N_CLUS)
    orders = jax.vmap(lambda one_key: jax.random.permutation(one_key, NB))(shuffle_keys).astype(jnp.int32)
    by_position = jnp.take_along_axis(by_position, orders, axis=1)
    source_perm = jax.random.permutation(keys[6], N_CLUS).astype(jnp.int32)
    inverse = jnp.argsort(source_perm, stable=True)
    return by_position[inverse]


def draw_block_cluster(key, part):
    row_keys = jax.random.split(jax.random.fold_in(key, 11), N_DP)
    table = jax.vmap(draw_row_routes)(row_keys)
    return table.reshape(BLOCKS, 1).astype(jnp.int32)


def touch_ends(values, key, smallest, top_value):
    place = [jax.random.randint(jax.random.fold_in(key, axis), (), 0, length) for axis, length in enumerate(values.shape)]
    widest = values.shape.index(max(values.shape))
    neighbour = place[:widest] + [(place[widest] + 1) % values.shape[widest]] + place[widest + 1:]
    return values.at[tuple(place)].set(smallest).at[tuple(neighbour)].set(top_value)


def block_levels(key, shape, shards, low, top_value):
    factor_of, own = 1.0, jax.random.fold_in(key, 6)
    for dim, blocks in shards:
        steps = jnp.exp(jax.random.uniform(jax.random.fold_in(own, dim), (blocks,), jnp.float32, low / len(shards), top_value / len(shards)))
        factor_of = factor_of * jnp.repeat(steps, shape[dim] // blocks).reshape([-1 if axis == dim else 1 for axis in range(len(shape))])
    return factor_of


def normal_values(stream_key, dims, scale, bound, shards=(), kind=jnp.bfloat16):
    values = scale * jax.random.normal(stream_key, dims, jnp.float32)
    if shards:
        values = values * block_levels(stream_key, dims, shards, -0.22, 0.18)
    return jnp.clip(values, -bound, bound).astype(kind)


def setup_inputs(seed: int = 0) -> dict:
    splits = jax.random.split(jax.random.key(seed), 5)
    return {
        "points": draw_points(jax.random.fold_in(splits[4], 71), 0),
        "block_cluster": draw_block_cluster(jax.random.fold_in(splits[4], 71), 0),
        "queries": normal_values(splits[2], (NQ, D), 1.0, 6.0, ((0, 32),)),
        "query_ids": touch_ends(jax.random.randint(splits[3], (CLUSTERS, MQ), 0, NQ), jax.random.fold_in(splits[3], 1), 0, NQ - 1).astype(jnp.int32),
    }


def reference(points, block_cluster, queries, query_ids):

    def add_block(index, carry):
        gram_acc, cross_acc = carry
        which = block_cluster[index, 0].astype(jnp.int32)
        block = lax.dynamic_index_in_dim(points, index, 0, keepdims=False)
        wanted = lax.dynamic_index_in_dim(query_ids, which, 0, keepdims=False).astype(jnp.int32)
        train_rows = queries[wanted]
        row_weight = lax.rsqrt(lax.optimization_barrier(jnp.mean(jnp.square(block.astype(jnp.float32)), axis=1)) + 1e-06)
        raw = jnp.dot(train_rows, block.T, preferred_element_type=jnp.float32)
        scores = (raw * row_weight[None, :]).astype(jnp.bfloat16)
        gram_acc = gram_acc.at[which].add(jnp.dot(block.T, block, preferred_element_type=jnp.float32))
        cross_acc = cross_acc.at[which].add(jnp.dot(block.T, scores.T, preferred_element_type=jnp.float32))
        return (gram_acc, cross_acc)
    gram_init = jnp.zeros((CLUSTERS, D, D), jnp.float32)
    cross_init = jnp.zeros((CLUSTERS, D, MQ), jnp.float32)
    gram_acc, cross_acc = lax.fori_loop(0, BLOCKS, add_block, (gram_init, cross_init))
    factor = 1.0 / MEANROWS
    return (gram_acc * factor, cross_acc * factor)
```

```python
import functools

import jax
import jax.numpy as jnp
from jax import lax
from jax.experimental import pallas as pl
from jax.experimental.pallas import tpu as pltpu
from jax.sharding import PartitionSpec as P

MEANROWS = 256
PIECE = 16
PAIR_CAP = 3
AXES = ("dp", "clus")
ANY = pl.BlockSpec(memory_space=pl.ANY)
SMEM = pl.BlockSpec(memory_space=pltpu.SMEM)
VMEM = pl.BlockSpec(memory_space=pltpu.VMEM)


def gather_labels(labels):
    table = labels.reshape(1, -1)
    for axis in ("clus", "dp"):
        count, here = lax.axis_size(axis), lax.axis_index(axis)
        bit = 1
        while bit < count:
            other = lax.ppermute(table, axis, [(i, i ^ bit) for i in range(count)])
            lower = (here & bit) == 0
            table = jnp.where(
                lower, jnp.concatenate([table, other]), jnp.concatenate([other, table])
            )
            bit *= 2
    return table.reshape(-1)


def send_kernel(n_dp, n_clus, cl_own, count, place, labels, pieces, *rest):
    sends, (used, sems) = rest[: n_dp - 1], rest[n_dp - 1 :]
    row = place[0]
    for hop in range(n_dp):
        used[hop] = 0

    def hop_of(i):
        target = labels[row * count + i] // (cl_own * n_clus)
        return lax.rem(target - row + n_dp, n_dp)

    def start(i, carry):
        hop = hop_of(i)
        slot = used[hop]
        used[hop] = slot + 1
        for d in range(1, n_dp):

            @pl.when(hop == d)
            def _():
                pltpu.make_async_copy(pieces.at[i], sends[d - 1].at[slot], sems.at[i]).start()

        return carry

    def finish(i, carry):
        @pl.when(hop_of(i) != 0)
        def _():
            pltpu.make_async_copy(pieces.at[i], sends[0].at[0], sems.at[i]).wait()

        return carry

    lax.fori_loop(0, count, start, 0)
    lax.fori_loop(0, count, finish, 0)


def pack_to_owners(n_dp, n_clus, cl_own, count, hops, slots, place, labels, *rest):
    sources, (out, used, sems) = rest[: len(hops)], rest[len(hops) :]
    row = place[0]
    for i in range(n_clus * cl_own):
        used[i] = 0

    for k, hop in enumerate(hops):
        source_row = lax.rem(row - hop + n_dp, n_dp)

        def start(i, arrived):
            label = labels[source_row * count + i]
            mine = label // (cl_own * n_clus) == row

            @pl.when(mine)
            def _():
                local = lax.rem(label, cl_own * n_clus)
                seen = used[local]
                used[local] = seen + 1
                slot = jnp.where(lax.rem(label, cl_own) == 0, seen, slots - 1 - seen)
                at = i if hop == 0 else arrived
                pltpu.make_async_copy(
                    sources[k].at[at], out.at[local // cl_own, slot], sems.at[k, i]
                ).start()

            return arrived + mine.astype(jnp.int32)

        lax.fori_loop(0, count, start, 0)

    for k, hop in enumerate(hops):
        source_row = lax.rem(row - hop + n_dp, n_dp)

        def finish(i, carry):
            @pl.when(labels[source_row * count + i] // (cl_own * n_clus) == row)
            def _():
                pltpu.make_async_copy(sources[k].at[0], out.at[0, 0], sems.at[k, i]).wait()

            return carry

        lax.fori_loop(0, count, finish, 0)


def terms_kernel(
    cl_own, slots, fsplit, counts, ids, table, first, second, gram, cross,
    rows, gram_acc, cross_acc, row_sems, out_sems,
):
    cap, width = rows.shape[1] - 1, rows.shape[-1]
    part = width // fsplit
    groups = (first, second)

    def copies(owned, g, k):
        slot = k if owned == 0 else slots - 1 - k
        block = k if g == 0 else counts[owned] + k
        return [
            pltpu.make_async_copy(
                groups[g].at[:, f, slot],
                rows.at[owned, block, :, :, pl.ds(f * part, part)],
                row_sems.at[owned, g, k, f],
            )
            for f in range(fsplit)
        ]

    def each(owned, act):
        for g in range(2):

            def body(k, carry):
                for copy in copies(owned, g, k):
                    act(copy)
                return carry

            lax.fori_loop(0, counts[g * cl_own + owned], body, 0)

    for owned in range(cl_own):
        each(owned, lambda copy: copy.start())
    for owned in range(cl_own):
        total = counts[owned] + counts[cl_own + owned]
        rows[owned, total] = jnp.zeros(rows.shape[2:], rows.dtype)

        wanted = ids[owned][:, None]
        columns = lax.broadcasted_iota(jnp.int32, (ids.shape[1], table.shape[0]), 1)
        chosen = jnp.where(columns == wanted, 1.0, 0.0).astype(jnp.bfloat16)
        train = jnp.dot(chosen, table[...], preferred_element_type=jnp.float32)
        train = train.astype(jnp.bfloat16)
        gram_acc[owned] = jnp.zeros(gram_acc.shape[1:], jnp.float32)
        cross_acc[owned] = jnp.zeros(cross_acc.shape[1:], jnp.float32)
        each(owned, lambda copy: copy.wait())

        def pair(step, carry):
            block = rows[owned, pl.ds(2 * step, 2)].reshape(-1, width)
            wide = block.astype(jnp.float32)
            squares = jnp.sum(wide * wide, axis=1, keepdims=True)
            weight = lax.rsqrt(squares / width + 1e-06)
            raw = lax.dot_general(
                block, train, (((1,), (1,)), ((), ())), preferred_element_type=jnp.float32
            )
            scores = (raw * weight).astype(jnp.bfloat16)
            over_rows = (((0,), (0,)), ((), ()))
            cross_acc[owned] += (1.0 / MEANROWS) * lax.dot_general(
                block, scores, over_rows, preferred_element_type=jnp.float32
            )
            gram_acc[owned] += (1.0 / MEANROWS) * lax.dot_general(
                block, block, over_rows, preferred_element_type=jnp.float32
            )
            return carry

        lax.fori_loop(0, (total + 1) // 2, pair, 0)
        pltpu.make_async_copy(gram_acc.at[owned], gram.at[owned], out_sems.at[0, owned]).start()
        pltpu.make_async_copy(cross_acc.at[owned], cross.at[owned], out_sems.at[1, owned]).start()
    for owned in range(cl_own):
        pltpu.make_async_copy(gram_acc.at[owned], gram.at[owned], out_sems.at[0, owned]).wait()
        pltpu.make_async_copy(cross_acc.at[owned], cross.at[owned], out_sems.at[1, owned]).wait()


def local(points, block_cluster, queries, query_ids):
    n_clus, n_dp = lax.axis_size("clus"), lax.axis_size("dp")
    nb, blk_rows, width = points.shape
    cl_own, mq = query_ids.shape
    assert cl_own == 2
    fsplit = max(1, n_clus * PIECE // blk_rows)
    part = width // fsplit
    groups = blk_rows // PIECE
    count = n_clus * nb
    row, col = lax.axis_index("dp"), lax.axis_index("clus")

    table = lax.all_gather(queries, AXES, axis=0, tiled=True)
    labels = gather_labels(block_cluster[:, 0])
    place = jnp.stack([row, col]).astype(jnp.int32)

    pieces = points.reshape(nb, groups, PIECE, fsplit, part).transpose(1, 3, 0, 2, 4)
    pieces = lax.all_to_all(
        pieces.reshape(n_clus, nb, PIECE, part), "clus", split_axis=0, concat_axis=0, tiled=True
    ).reshape(count, PIECE, part)

    near = tuple(range(n_dp // 2))
    far = tuple(range(n_dp // 2, n_dp))
    slots = PAIR_CAP * (n_dp // 2)

    row_of = lax.broadcasted_iota(jnp.int32, (n_dp * count,), 0) // count
    to_row = labels // (cl_own * n_clus)
    hop_of = (to_row - row_of) % n_dp
    pair_of = jnp.where(hop_of > 0, row_of * n_dp + hop_of, -1)
    pairs = lax.broadcasted_iota(jnp.int32, (n_dp * n_dp, 1), 0)
    most = jnp.max(jnp.sum((pair_of[None, :] == pairs).astype(jnp.int32), axis=1))

    mine = labels // cl_own == row * n_clus + col
    group_of = jnp.where((row - row_of) % n_dp < n_dp // 2, 0, cl_own)
    kind = jnp.where(mine, group_of + labels % cl_own, -1)
    kinds = lax.broadcasted_iota(jnp.int32, (2 * cl_own, 1), 0)
    counts = jnp.sum((kind[None, :] == kinds).astype(jnp.int32), axis=1)

    def packed(hops, place, labels, sources):
        return pl.pallas_call(
            functools.partial(pack_to_owners, n_dp, n_clus, cl_own, count, hops, slots),
            out_shape=jax.ShapeDtypeStruct((n_clus, slots, PIECE, part), points.dtype),
            in_specs=[SMEM, SMEM] + [ANY] * len(hops),
            out_specs=ANY,
            scratch_shapes=[
                pltpu.SMEM((n_clus * cl_own,), jnp.int32),
                pltpu.SemaphoreType.DMA((len(hops), count)),
            ],
        )(place, labels, *sources)

    def to_owners(sent):
        return lax.all_to_all(sent, "clus", split_axis=0, concat_axis=0, tiled=True)

    def route(cap):
        def run(place, labels, pieces):
            sends = pl.pallas_call(
                functools.partial(send_kernel, n_dp, n_clus, cl_own, count),
                out_shape=[jax.ShapeDtypeStruct((cap, PIECE, part), points.dtype)] * (n_dp - 1),
                in_specs=[SMEM, SMEM, ANY],
                out_specs=[ANY] * (n_dp - 1),
                scratch_shapes=[
                    pltpu.SMEM((n_dp,), jnp.int32),
                    pltpu.SemaphoreType.DMA((count,)),
                ],
            )(place, labels, pieces)
            arrived = [pieces] + [
                lax.ppermute(sends[d - 1], "dp", [(i, (i + d) % n_dp) for i in range(n_dp)])
                for d in range(1, n_dp)
            ]
            first = to_owners(packed(near, place, labels, [arrived[d] for d in near]))
            second = to_owners(packed(far, place, labels, [arrived[d] for d in far]))
            return first, second

        return run

    largest = min(PAIR_CAP * n_clus, count)
    levels = [c for c in (9, 10, 11, 12, 14, 18) if c < largest] + [largest]
    which = jnp.sum((most > jnp.array(levels[:-1], jnp.int32)).astype(jnp.int32))
    first, second = lax.switch(which, [route(c) for c in levels], place, labels, pieces)

    cap = PAIR_CAP * n_dp
    shape = (groups, fsplit, slots, PIECE, part)
    gram, cross = pl.pallas_call(
        functools.partial(terms_kernel, cl_own, slots, fsplit),
        out_shape=[
            jax.ShapeDtypeStruct((cl_own, width, width), jnp.float32),
            jax.ShapeDtypeStruct((cl_own, width, mq), jnp.float32),
        ],
        in_specs=[SMEM, VMEM, VMEM, ANY, ANY],
        out_specs=[ANY, ANY],
        scratch_shapes=[
            pltpu.VMEM((cl_own, cap + 1, groups, PIECE, width), points.dtype),
            pltpu.VMEM((cl_own, width, width), jnp.float32),
            pltpu.VMEM((cl_own, width, mq), jnp.float32),
            pltpu.SemaphoreType.DMA((cl_own, 2, slots, fsplit)),
            pltpu.SemaphoreType.DMA((2, cl_own)),
        ],
        compiler_params=pltpu.CompilerParams(vmem_limit_bytes=48 * 2**20),
    )(counts, query_ids, table, first.reshape(shape), second.reshape(shape))
    return gram, cross


def solution(mesh):
    placed = (
        P(AXES, None, None),
        P(AXES, None),
        P(AXES, None),
        P(AXES, None),
    )
    return jax.shard_map(
        local,
        mesh=mesh,
        in_specs=placed,
        out_specs=(P(AXES, None, None), P(AXES, None, None)),
        check_vma=False,
    )
```

```python
import functools

import jax
import jax.numpy as jnp
from jax import lax
from jax.experimental import pallas as pl
from jax.experimental.pallas import tpu as pltpu
from jax.sharding import PartitionSpec as P

MEANROWS = 256
PIECE = 16
LANES = 128
DIGIT = 128
PAIR_CAP = 3
HOP_SLOTS = 12
AXES = ("dp", "clus")
ANY = pl.BlockSpec(memory_space=pl.ANY)
SMEM = pl.BlockSpec(memory_space=pltpu.SMEM)
VMEM = pl.BlockSpec(memory_space=pltpu.VMEM)


def slice_kernel(n_clus, fsplit, labels, points, queries, out, ask):
    nb, _, width = points.shape
    blocks = width // fsplit // LANES
    lane = lax.broadcasted_iota(jnp.int32, (PIECE, LANES), 1)
    tile = jnp.zeros((PIECE, LANES), jnp.float32)
    for b in range(nb):
        label = labels[b]
        tile = jnp.where(lane == 2 * b, (label // DIGIT).astype(jnp.float32), tile)
        tile = jnp.where(lane == 2 * b + 1, lax.rem(label, DIGIT).astype(jnp.float32), tile)
    tile = tile.astype(out.dtype)
    for q in range(n_clus):
        group, part = q // fsplit, q % fsplit
        for b in range(nb):
            for k in range(blocks):
                out[q, pl.ds((b * blocks + k) * PIECE, PIECE), :] = points[
                    b, pl.ds(group * PIECE, PIECE), pl.ds((part * blocks + k) * LANES, LANES)
                ]
        out[q, pl.ds(nb * blocks * PIECE, PIECE), :] = tile
    rows = queries.shape[0]
    for k in range(width // LANES):
        ask[pl.ds(k * rows, rows), :] = queries[:, pl.ds(k * LANES, LANES)]
    ask[pl.ds(width // LANES * rows, PIECE), :] = tile


def send_kernel(n_dp, n_clus, cl_own, nb, cap, place, labels, pieces, *rest):
    asks, sends, (own, used, filled) = rest[:n_dp], rest[n_dp : 2 * n_dp - 1], rest[2 * n_dp - 1 :]
    row = place[0]
    size = (pieces.shape[1] - PIECE) // nb
    for hop in range(n_dp):
        used[hop] = 0
    for i in range(n_clus * cl_own):
        filled[i] = 0

    def one(q, carry):
        for b in range(nb):
            label = labels[q * nb + b]
            hop = lax.rem(label // (cl_own * n_clus) - row + n_dp, n_dp)
            slot = used[hop]
            used[hop] = slot + 1
            for d in range(1, n_dp):

                @pl.when((hop == d) & (slot < cap))
                def _():
                    at = pl.multiple_of(slot * size, size)
                    sends[d - 1][pl.ds(at, size), :] = pieces[q, pl.ds(b * size, size), :]

            @pl.when(hop == 0)
            def _():
                local = lax.rem(label, cl_own * n_clus)
                seen = filled[local]
                filled[local] = seen + 1
                mine = jnp.where(lax.rem(label, cl_own) == 0, seen, PAIR_CAP - 1 - seen)
                at = pl.multiple_of(mine * size, size)
                own[local // cl_own, pl.ds(at, size), :] = pieces[q, pl.ds(b * size, size), :]

        return carry

    lax.fori_loop(0, n_clus, one, 0)
    length = asks[0].shape[0] - PIECE
    sub = lax.broadcasted_iota(jnp.int32, (PIECE, LANES), 0)
    tile = jnp.zeros((PIECE, LANES), jnp.float32)
    for d in range(n_dp):
        tile = jnp.where(sub == d, asks[d][pl.ds(length, PIECE), :].astype(jnp.float32), tile)
    tile = tile.astype(own.dtype)
    base = PAIR_CAP * size
    for q in range(n_clus):
        for d in range(n_dp):
            own[q, pl.ds(base + d * length, length), :] = asks[d][pl.ds(0, length), :]
        own[q, pl.ds(base + n_dp * length, PIECE), :] = tile


def owner_kernel(n_dp, n_clus, cl_own, nb, cap, slots, size, place, labels, *rest):
    sources, (out, used) = rest[: n_dp - 1], rest[n_dp - 1 :]
    row = place[0]
    count = n_clus * nb
    for i in range(n_clus * cl_own):
        used[i] = 0

    for hop in range(1, n_dp):

        def one(q, arrived):
            for b in range(nb):
                label = labels[hop * count + q * nb + b]
                mine = label // (cl_own * n_clus) == row

                @pl.when(mine & (arrived < cap))
                def _():
                    local = lax.rem(label, cl_own * n_clus)
                    seen = used[local]
                    used[local] = seen + 1
                    slot = jnp.where(lax.rem(label, cl_own) == 0, seen, slots - 1 - seen)
                    at = pl.multiple_of(arrived * size, size)
                    out[local // cl_own, slot] = sources[hop - 1][pl.ds(at, size), :]

                arrived += mine.astype(jnp.int32)
            return arrived

        lax.fori_loop(0, n_clus, one, jnp.int32(0))


def terms_kernel(
    cl_own, fsplit, counts, ids, order, first, second, gram, cross,
    rows, gram_acc, cross_acc, out_sems,
):
    tiles, groups = rows.shape[1], rows.shape[3]
    width = tiles * LANES
    per_part = tiles // fsplit
    size = per_part * PIECE
    n_clus, entries = first.shape[0], order.shape[1]
    slots = second.shape[1]

    asked = first[:, pl.ds(PAIR_CAP * size, entries * tiles // n_clus), :]
    asked = asked.reshape(-1, tiles, PIECE, LANES)
    table = jnp.concatenate([asked[:, t].reshape(entries, LANES) for t in range(tiles)], axis=1)

    for owned in range(cl_own):
        total = counts[owned] + counts[cl_own + owned]

        def place_block(block, piece):
            for q in range(n_clus):
                group, part = q // fsplit, q % fsplit
                for t in range(per_part):
                    rows[owned, part * per_part + t, block, group] = piece(q, t)

        def place_first(k, carry):
            slot = k if owned == 0 else PAIR_CAP - 1 - k
            at = pl.multiple_of(slot * size, size)
            place_block(k, lambda q, t: first[q, pl.ds(at + t * PIECE, PIECE), :])
            return carry

        def place_second(k, carry):
            slot = k if owned == 0 else slots - 1 - k
            place_block(
                counts[owned] + k, lambda q, t: second[q, slot, pl.ds(t * PIECE, PIECE), :]
            )
            return carry

        lax.fori_loop(0, counts[owned], place_first, 0)
        lax.fori_loop(0, counts[cl_own + owned], place_second, 0)
        for t in range(tiles):
            rows[owned, t, total] = jnp.zeros(rows.shape[3:], rows.dtype)

        chosen = jnp.where(order[...] == ids[owned][:, None], 1.0, 0.0).astype(jnp.bfloat16)
        train = jnp.dot(chosen, table, preferred_element_type=jnp.float32)
        train = train.astype(jnp.bfloat16)
        gram_acc[owned] = jnp.zeros(gram_acc.shape[1:], jnp.float32)
        cross_acc[owned] = jnp.zeros(cross_acc.shape[1:], jnp.float32)

        def pair(step, carry):
            block = jnp.concatenate(
                [rows[owned, t, pl.ds(2 * step, 2)].reshape(-1, LANES) for t in range(tiles)],
                axis=1,
            )
            wide = block.astype(jnp.float32)
            squares = jnp.sum(wide * wide, axis=1, keepdims=True)
            weight = lax.rsqrt(squares / width + 1e-06)
            raw = lax.dot_general(
                block, train, (((1,), (1,)), ((), ())), preferred_element_type=jnp.float32
            )
            scores = (raw * weight).astype(jnp.bfloat16)
            over_rows = (((0,), (0,)), ((), ()))
            cross_acc[owned] += (1.0 / MEANROWS) * lax.dot_general(
                block, scores, over_rows, preferred_element_type=jnp.float32
            )
            gram_acc[owned] += (1.0 / MEANROWS) * lax.dot_general(
                block, block, over_rows, preferred_element_type=jnp.float32
            )
            return carry

        lax.fori_loop(0, (total + 1) // 2, pair, 0)
        pltpu.make_async_copy(gram_acc.at[owned], gram.at[owned], out_sems.at[0, owned]).start()
        pltpu.make_async_copy(cross_acc.at[owned], cross.at[owned], out_sems.at[1, owned]).start()
    for owned in range(cl_own):
        pltpu.make_async_copy(gram_acc.at[owned], gram.at[owned], out_sems.at[0, owned]).wait()
        pltpu.make_async_copy(cross_acc.at[owned], cross.at[owned], out_sems.at[1, owned]).wait()


def local(points, block_cluster, queries, query_ids):
    n_clus, n_dp = lax.axis_size("clus"), lax.axis_size("dp")
    nb, blk_rows, width = points.shape
    cl_own, mq = query_ids.shape
    nq = queries.shape[0]
    assert cl_own == 2 and max(n_clus, n_dp) <= PIECE and nq == PIECE
    fsplit = max(1, n_clus * PIECE // blk_rows)
    groups = blk_rows // PIECE
    size = PIECE * width // fsplit // LANES
    length = nq * width // LANES
    count = n_clus * nb
    dtype = points.dtype
    row, col = lax.axis_index("dp"), lax.axis_index("clus")
    place = row.astype(jnp.int32).reshape(1)

    def to_plane(sent):
        return lax.all_to_all(sent, "clus", split_axis=0, concat_axis=0, tiled=True)

    def along_dp(sent, hop):
        return lax.ppermute(sent, "dp", [(i, (i + hop) % n_dp) for i in range(n_dp)])

    def read_labels(tile):
        digits = tile[..., : 2 * nb].astype(jnp.int32)
        return digits[..., 0::2] * DIGIT + digits[..., 1::2]

    sliced, ask = pl.pallas_call(
        functools.partial(slice_kernel, n_clus, fsplit),
        out_shape=[
            jax.ShapeDtypeStruct((n_clus, nb * size + PIECE, LANES), dtype),
            jax.ShapeDtypeStruct((length + PIECE, LANES), dtype),
        ],
        in_specs=[SMEM, VMEM, VMEM],
        out_specs=[VMEM, VMEM],
    )(block_cluster[:, 0], points, queries)
    pieces = to_plane(sliced)
    asks = [ask] + [along_dp(ask, d) for d in range(1, n_dp)]
    plane_labels = read_labels(pieces[:, nb * size, :]).reshape(count)

    def cross_planes(cap, plane_labels, pieces, asks):
        *sends, own = pl.pallas_call(
            functools.partial(send_kernel, n_dp, n_clus, cl_own, nb, cap),
            out_shape=[jax.ShapeDtypeStruct((cap * size, LANES), dtype)] * (n_dp - 1)
            + [
                jax.ShapeDtypeStruct((n_clus, PAIR_CAP * size + n_dp * length + PIECE, LANES), dtype)
            ],
            in_specs=[SMEM, SMEM, VMEM] + [VMEM] * n_dp,
            out_specs=[VMEM] * n_dp,
            scratch_shapes=[
                pltpu.SMEM((n_dp,), jnp.int32),
                pltpu.SMEM((n_clus * cl_own,), jnp.int32),
            ],
        )(place, plane_labels, pieces, *asks)
        return [along_dp(sends[d - 1], d) for d in range(1, n_dp)], own

    largest = min(PAIR_CAP * n_clus, count)
    cap = min(HOP_SLOTS * n_clus // 8, largest)
    arrived, own = cross_planes(cap, plane_labels, pieces, asks)
    first = to_plane(own)

    tail = first[:, PAIR_CAP * size + n_dp * length :, :][:, :n_dp]
    labels = read_labels(tail).transpose(1, 0, 2).reshape(n_dp, count)
    hop = lax.broadcasted_iota(jnp.int32, (n_dp, count), 0)
    to_row = labels // (cl_own * n_clus)
    hops_to_go = (to_row - row + hop) % n_dp
    pair_of = jnp.where(hops_to_go > 0, hop * n_dp + hops_to_go, -1).reshape(1, -1)
    pairs = lax.broadcasted_iota(jnp.int32, (n_dp * n_dp, 1), 0)
    most = jnp.max(jnp.sum((pair_of == pairs).astype(jnp.int32), axis=1))
    owner_of = jnp.where(hops_to_go > 0, labels // cl_own, -1).reshape(1, -1)
    owners = lax.broadcasted_iota(jnp.int32, (n_dp * n_clus, 1), 0)
    busiest = jnp.max(jnp.sum((owner_of == owners).astype(jnp.int32), axis=1))

    mine = labels // cl_own == row * n_clus + col
    kind = jnp.where(mine, jnp.where(hop == 0, 0, cl_own) + labels % cl_own, -1)
    kinds = lax.broadcasted_iota(jnp.int32, (2 * cl_own, 1), 0)
    counts = jnp.sum((kind.reshape(1, -1) == kinds).astype(jnp.int32), axis=1)

    entry = jnp.arange(n_clus * n_dp * nq, dtype=jnp.int32)
    behind = (row - entry // nq) % n_dp
    order = ((behind * n_clus + entry // (n_dp * nq)) * nq + entry % nq).reshape(1, -1)

    flat_labels = labels.reshape(-1)

    def finish(slots, cap, counts, order, flat_labels, first, arrived):
        packed = pl.pallas_call(
            functools.partial(owner_kernel, n_dp, n_clus, cl_own, nb, cap, slots, size),
            out_shape=jax.ShapeDtypeStruct((n_clus, slots, size, LANES), dtype),
            in_specs=[SMEM, SMEM] + [VMEM] * (n_dp - 1),
            out_specs=VMEM,
            scratch_shapes=[pltpu.SMEM((n_clus * cl_own,), jnp.int32)],
        )(place, flat_labels, *arrived)
        second = to_plane(packed)
        blocks = PAIR_CAP * n_dp + 1
        return pl.pallas_call(
            functools.partial(terms_kernel, cl_own, fsplit),
            out_shape=[
                jax.ShapeDtypeStruct((cl_own, width, width), jnp.float32),
                jax.ShapeDtypeStruct((cl_own, width, mq), jnp.float32),
            ],
            in_specs=[SMEM] + [VMEM] * 4,
            out_specs=[ANY, ANY],
            scratch_shapes=[
                pltpu.VMEM((cl_own, width // LANES, blocks, groups, PIECE, LANES), dtype),
                pltpu.VMEM((cl_own, width, width), jnp.float32),
                pltpu.VMEM((cl_own, width, mq), jnp.float32),
                pltpu.SemaphoreType.DMA((2, cl_own)),
            ],
            compiler_params=pltpu.CompilerParams(vmem_limit_bytes=44 * 2**20),
        )(counts, query_ids, order, first, second)

    most_slots = PAIR_CAP * (n_dp - 1)
    levels = [c for c in (5, 6, 7) if c < most_slots] + [most_slots]

    def level(slots):
        def run(counts, order, flat_labels, first, arrived, plane_labels, pieces, asks):
            return tuple(finish(slots, cap, counts, order, flat_labels, first, arrived))

        return run

    def full_route(counts, order, flat_labels, first, arrived, plane_labels, pieces, asks):
        arrived, _ = cross_planes(largest, plane_labels, pieces, asks)
        return tuple(finish(most_slots, largest, counts, order, flat_labels, first, arrived))

    which = jnp.sum((busiest > jnp.array(levels[:-1], jnp.int32)).astype(jnp.int32))
    which = jnp.where(most > cap, len(levels), which)
    branches = [level(c) for c in levels] + [full_route]
    return lax.switch(
        which, branches, counts, order, flat_labels, first, arrived, plane_labels, pieces, asks
    )


def solution(mesh):
    placed = (
        P(AXES, None, None),
        P(AXES, None),
        P(AXES, None),
        P(AXES, None),
    )
    return jax.shard_map(
        local,
        mesh=mesh,
        in_specs=placed,
        out_specs=(P(AXES, None, None), P(AXES, None, None)),
        check_vma=False,
    )
```

```python
import functools

import jax
import jax.numpy as jnp
from jax import lax
from jax.experimental import pallas as pl
from jax.experimental.pallas import tpu as pltpu
from jax.sharding import PartitionSpec as P

MEANROWS = 256
PIECE = 16
LANES = 128
DIGIT = 128
PAIR_CAP = 3
HOP_SLOTS = 12
AXES = ("dp", "clus")
ANY = pl.BlockSpec(memory_space=pl.ANY)
SMEM = pl.BlockSpec(memory_space=pltpu.SMEM)
VMEM = pl.BlockSpec(memory_space=pltpu.VMEM)


def slice_kernel(n_clus, fsplit, labels, points, queries, out, ask):
    nb, _, width = points.shape
    blocks = width // fsplit // LANES
    lane = lax.broadcasted_iota(jnp.int32, (PIECE, LANES), 1)
    tile = jnp.zeros((PIECE, LANES), jnp.float32)
    for b in range(nb):
        label = labels[b]
        tile = jnp.where(lane == 2 * b, (label // DIGIT).astype(jnp.float32), tile)
        tile = jnp.where(lane == 2 * b + 1, lax.rem(label, DIGIT).astype(jnp.float32), tile)
    tile = tile.astype(out.dtype)
    for q in range(n_clus):
        group, part = q // fsplit, q % fsplit
        for b in range(nb):
            for k in range(blocks):
                out[q, pl.ds((b * blocks + k) * PIECE, PIECE), :] = points[
                    b, pl.ds(group * PIECE, PIECE), pl.ds((part * blocks + k) * LANES, LANES)
                ]
        out[q, pl.ds(nb * blocks * PIECE, PIECE), :] = tile
    rows = queries.shape[0]
    for k in range(width // LANES):
        ask[pl.ds(k * rows, rows), :] = queries[:, pl.ds(k * LANES, LANES)]
    ask[pl.ds(width // LANES * rows, PIECE), :] = tile


def quotient(value, by):
    if by & (by - 1):
        return lax.div(value, by)
    return lax.shift_right_logical(value, by.bit_length() - 1)


def remainder(value, by):
    return lax.rem(value, by) if by & (by - 1) else lax.bitwise_and(value, by - 1)


def send_kernel(n_dp, n_clus, nb, cap, routes, pieces, *rest):
    sends, (used,) = rest[: n_dp - 1], rest[n_dp - 1 :]
    size = (pieces.shape[1] - PIECE) // nb
    for hop in range(n_dp):
        used[hop] = 0

    def one(q, carry):
        for b in range(nb):
            hop = quotient(routes[q * nb + b], DIGIT)
            slot = used[hop]
            used[hop] = slot + 1
            at = pl.multiple_of(slot * size, size)
            for d in range(1, n_dp):

                @pl.when((hop == d) & (slot < cap))
                def _():
                    sends[d - 1][pl.ds(at, size), :] = pieces[q, pl.ds(b * size, size), :]

        return carry

    lax.fori_loop(0, n_clus, one, 0)


def own_kernel(n_dp, n_clus, cl_own, nb, routes, pieces, *rest):
    asks, (own, filled) = rest[:n_dp], rest[n_dp:]
    size = (pieces.shape[1] - PIECE) // nb
    for i in range(n_clus * cl_own):
        filled[i] = 0

    def one(q, carry):
        for b in range(nb):
            route = routes[q * nb + b]

            @pl.when(route < DIGIT)
            def _():
                seen = filled[route]
                filled[route] = seen + 1
                slot = jnp.where(remainder(route, cl_own) == 0, seen, PAIR_CAP - 1 - seen)
                at = pl.multiple_of(slot * size, size)
                own[quotient(route, cl_own), pl.ds(at, size), :] = pieces[
                    q, pl.ds(b * size, size), :
                ]

        return carry

    lax.fori_loop(0, n_clus, one, 0)
    length = asks[0].shape[0] - PIECE
    half = length // 2
    sub = lax.broadcasted_iota(jnp.int32, (PIECE, LANES), 0)
    tile = jnp.zeros((PIECE, LANES), jnp.float32)
    for d in range(n_dp):
        tile = jnp.where(sub == d, asks[d][pl.ds(length, PIECE), :].astype(jnp.float32), tile)
    tile = tile.astype(own.dtype)
    base = PAIR_CAP * size
    for q in range(n_clus):
        for d in range(n_dp):
            own[q, pl.ds(base + d * half, half), :] = asks[d][pl.ds(q % 2 * half, half), :]
        own[q, pl.ds(base + n_dp * half, PIECE), :] = tile


def first_kernel(n_dp, n_clus, cl_own, nb, cap, routes, pieces, *rest):
    asks, sends, (own, used, filled) = rest[:n_dp], rest[n_dp : 2 * n_dp - 1], rest[2 * n_dp - 1 :]
    send_kernel(n_dp, n_clus, nb, cap, routes, pieces, *sends, used)
    own_kernel(n_dp, n_clus, cl_own, nb, routes, pieces, *asks, own, filled)


HEAD = 16


def plan_kernel(n_dp, n_clus, cl_own, count, most_sent, place, labels, info, filled):
    row, col = place[0], place[1]
    plane = cl_own * n_clus
    per_chip = 2 * cl_own
    chip = quotient(col, 2)
    for i in range(plane):
        filled[i] = 0

    def tally(i, carry):
        label = labels[count + i]
        inside = remainder(label, plane)
        filled[inside] += (quotient(label, plane) == row).astype(jnp.int32)
        return carry

    lax.fori_loop(0, (n_dp - 1) * count, tally, 0)

    def near(i, seen):
        first = labels[i] - (row * n_clus + col) * cl_own
        return tuple(s + (first == c).astype(jnp.int32) for c, s in enumerate(seen))

    seen = lax.fori_loop(0, count, near, (jnp.int32(0),) * cl_own)
    for c in range(cl_own):
        info[c] = seen[c]
        info[cl_own + c] = filled[col * cl_own + c]
    for first in range(0, plane, per_chip):
        start = jnp.int32(0)
        for i in range(first, first + per_chip):
            held = filled[i]
            filled[i] = start
            start += held
    for c in range(cl_own):
        info[2 * cl_own + c] = filled[col * cl_own + c]

    for hop in range(1, n_dp):

        def one(i, arrived):
            label = labels[hop * count + i]
            mine = quotient(label, plane) == row

            @pl.when(mine)
            def _():
                inside = remainder(label, plane)
                slot = filled[inside]
                filled[inside] = slot + 1
                step = lax.bitwise_xor(quotient(inside, per_chip), chip)
                info[HEAD + (hop - 1) * most_sent + arrived] = step * DIGIT + slot

            return arrived + mine.astype(jnp.int32)

        info[3 * cl_own + hop - 1] = lax.fori_loop(0, count, one, jnp.int32(0))


def owner_kernel(n_dp, cl_own, chips, cap, most_sent, size, info, *rest):
    sources, outs = rest[: n_dp - 1], rest[n_dp - 1 :]
    for hop in range(1, n_dp):

        def one(k, carry):
            code = info[HEAD + (hop - 1) * most_sent + k]
            step, slot = quotient(code, DIGIT), remainder(code, DIGIT)
            at = pl.multiple_of(k * size, size)
            to = pl.multiple_of(slot * size, size)
            for e in range(chips):

                @pl.when(step == e)
                def _():
                    outs[e][pl.ds(to, size), :] = sources[hop - 1][pl.ds(at, size), :]

            return carry

        lax.fori_loop(0, jnp.minimum(info[3 * cl_own + hop - 1], cap), one, 0)


def terms_kernel(cl_own, fsplit, chips, place, info, ids, order, first, other, *rest):
    same, sibling, rest = rest[:chips], rest[chips : 2 * chips], rest[2 * chips :]
    gram, cross, rows, gram_acc, cross_acc, out_sems = rest
    tiles = rows.shape[1]
    width = tiles * LANES
    per_part = tiles // fsplit
    size = per_part * PIECE
    n_clus, entries = first.shape[0], order.shape[1]
    core = remainder(place[1], 2)

    def half_table(asked):
        asked = asked.reshape(-1, tiles // 2, PIECE, LANES)
        return jnp.concatenate(
            [asked[:, t].reshape(entries, LANES) for t in range(tiles // 2)], axis=1
        )

    here = half_table(first[:, pl.ds(PAIR_CAP * size, other.shape[1]), :])
    there = half_table(other[...])

    for owned in range(cl_own):
        near, far = info[owned], info[cl_own + owned]
        total = near + far

        def place_first(k, carry):
            slot = k if owned == 0 else PAIR_CAP - 1 - k
            at = pl.multiple_of(slot * size, size)
            for q in range(n_clus):
                group, part = q // fsplit, q % fsplit
                for t in range(per_part):
                    rows[owned, part * per_part + t, k, group] = first[
                        q, pl.ds(at + t * PIECE, PIECE), :
                    ]
            return carry

        def place_far(k, carry):
            at = pl.multiple_of((info[2 * cl_own + owned] + k) * size, size)
            for e in range(chips):
                for lane, source in enumerate((same[e], sibling[e])):
                    group = 2 * e + lane if fsplit == 1 else e
                    part = 0 if fsplit == 1 else lax.bitwise_xor(core, lane)
                    for t in range(per_part):
                        rows[owned, part * per_part + t, near + k, group] = source[
                            pl.ds(at + t * PIECE, PIECE), :
                        ]
            return carry

        lax.fori_loop(0, near, place_first, 0)
        lax.fori_loop(0, far, place_far, 0)
        for t in range(tiles):
            rows[owned, t, total] = jnp.zeros(rows.shape[3:], rows.dtype)

        chosen = jnp.where(order[...] == ids[owned][:, None], 1.0, 0.0).astype(jnp.bfloat16)
        train_here = jnp.dot(chosen, here, preferred_element_type=jnp.float32)
        train_there = jnp.dot(chosen, there, preferred_element_type=jnp.float32)
        train = jnp.where(
            core == 0,
            jnp.concatenate([train_here, train_there], axis=1),
            jnp.concatenate([train_there, train_here], axis=1),
        ).astype(jnp.bfloat16)
        gram_acc[owned] = jnp.zeros(gram_acc.shape[1:], jnp.float32)
        cross_acc[owned] = jnp.zeros(cross_acc.shape[1:], jnp.float32)

        def pair(step, carry):
            block = jnp.concatenate(
                [rows[owned, t, pl.ds(2 * step, 2)].reshape(-1, LANES) for t in range(tiles)],
                axis=1,
            )
            wide = block.astype(jnp.float32)
            squares = jnp.sum(wide * wide, axis=1, keepdims=True)
            weight = lax.rsqrt(squares / width + 1e-06)
            raw = lax.dot_general(
                block, train, (((1,), (1,)), ((), ())), preferred_element_type=jnp.float32
            )
            scores = (raw * weight).astype(jnp.bfloat16)
            over_rows = (((0,), (0,)), ((), ()))
            cross_acc[owned] += (1.0 / MEANROWS) * lax.dot_general(
                block, scores, over_rows, preferred_element_type=jnp.float32
            )
            gram_acc[owned] += (1.0 / MEANROWS) * lax.dot_general(
                block, block, over_rows, preferred_element_type=jnp.float32
            )
            return carry

        lax.fori_loop(0, (total + 1) // 2, pair, 0)
        pltpu.make_async_copy(gram_acc.at[owned], gram.at[owned], out_sems.at[0, owned]).start()
        pltpu.make_async_copy(cross_acc.at[owned], cross.at[owned], out_sems.at[1, owned]).start()
    for owned in range(cl_own):
        pltpu.make_async_copy(gram_acc.at[owned], gram.at[owned], out_sems.at[0, owned]).wait()
        pltpu.make_async_copy(cross_acc.at[owned], cross.at[owned], out_sems.at[1, owned]).wait()


def local(points, block_cluster, queries, query_ids):
    n_clus, n_dp = lax.axis_size("clus"), lax.axis_size("dp")
    nb, blk_rows, width = points.shape
    cl_own, mq = query_ids.shape
    nq = queries.shape[0]
    plane = cl_own * n_clus
    fsplit = max(1, n_clus * PIECE // blk_rows)
    chips = n_clus // 2
    assert cl_own == 2 and nq == PIECE and fsplit <= 2
    assert max(n_clus, n_dp) <= PIECE and plane <= DIGIT and 3 * cl_own + n_dp - 1 <= HEAD
    groups = blk_rows // PIECE
    size = PIECE * width // fsplit // LANES
    length = nq * width // LANES
    count = n_clus * nb
    dtype = points.dtype
    row = lax.axis_index("dp").astype(jnp.int32)
    col = lax.axis_index("clus").astype(jnp.int32)
    place = jnp.stack([row, col])

    def to_plane(sent):
        return lax.all_to_all(sent, "clus", split_axis=0, concat_axis=0, tiled=True)

    def along_dp(sent, hop):
        return lax.ppermute(sent, "dp", [(i, (i + hop) % n_dp) for i in range(n_dp)])

    def in_plane(sent, bits):
        return lax.ppermute(sent, "clus", [(i, i ^ bits) for i in range(n_clus)])

    def read_labels(tile):
        digits = tile[..., : 2 * nb].astype(jnp.int32)
        return digits[..., 0::2] * DIGIT + digits[..., 1::2]

    def shape_of(*dims):
        return jax.ShapeDtypeStruct(dims, dtype)

    sliced, ask = pl.pallas_call(
        functools.partial(slice_kernel, n_clus, fsplit),
        out_shape=[
            shape_of(n_clus, nb * size + PIECE, LANES),
            shape_of(length + PIECE, LANES),
        ],
        in_specs=[SMEM, VMEM, VMEM],
        out_specs=[VMEM, VMEM],
    )(block_cluster[:, 0], points, queries)
    pieces = to_plane(sliced)
    asks = [ask] + [along_dp(ask, d) for d in range(1, n_dp)]

    largest = min(PAIR_CAP * n_clus, count)
    cap = min(HOP_SLOTS * n_clus // 8, largest)
    plane_labels = read_labels(pieces[:, nb * size, :]).reshape(count)
    routes = (plane_labels // plane - row) % n_dp * DIGIT + plane_labels % plane

    def cross_planes(cap, routes, pieces):
        sends = pl.pallas_call(
            functools.partial(send_kernel, n_dp, n_clus, nb, cap),
            out_shape=[shape_of(cap * size, LANES)] * (n_dp - 1),
            in_specs=[SMEM, VMEM],
            out_specs=[VMEM] * (n_dp - 1),
            scratch_shapes=[pltpu.SMEM((n_dp,), jnp.int32)],
        )(routes, pieces)
        return [along_dp(sends[d - 1], d) for d in range(1, n_dp)]

    *sends, own = pl.pallas_call(
        functools.partial(first_kernel, n_dp, n_clus, cl_own, nb, cap),
        out_shape=[shape_of(cap * size, LANES)] * (n_dp - 1)
        + [shape_of(n_clus, PAIR_CAP * size + n_dp * length // 2 + PIECE, LANES)],
        in_specs=[SMEM] + [VMEM] * (1 + n_dp),
        out_specs=[VMEM] * n_dp,
        scratch_shapes=[pltpu.SMEM((n_dp,), jnp.int32), pltpu.SMEM((plane,), jnp.int32)],
    )(routes, pieces, *asks)
    arrived = [along_dp(sends[d - 1], d) for d in range(1, n_dp)]
    first = to_plane(own)
    base = PAIR_CAP * size
    other = in_plane(first[:, base : base + n_dp * length // 2], 1)

    labels = read_labels(first[:, base + n_dp * length // 2 :][:, :n_dp])
    labels = labels.transpose(1, 0, 2).reshape(n_dp, count)
    hop = lax.broadcasted_iota(jnp.int32, (n_dp, count), 0)
    hops_to_go = (labels // plane - row + hop) % n_dp
    pair_of = jnp.where(hops_to_go > 0, hop * n_dp + hops_to_go, -1).reshape(1, -1)
    pairs = lax.broadcasted_iota(jnp.int32, (n_dp * n_dp, 1), 0)
    most = jnp.max(jnp.sum((pair_of == pairs).astype(jnp.int32), axis=1))
    chip_of = jnp.where(hops_to_go > 0, labels // (2 * cl_own), -1).reshape(1, -1)
    all_chips = lax.broadcasted_iota(jnp.int32, (n_dp * chips, 1), 0)
    busiest = jnp.max(jnp.sum((chip_of == all_chips).astype(jnp.int32), axis=1))

    info = pl.pallas_call(
        functools.partial(plan_kernel, n_dp, n_clus, cl_own, count, largest),
        out_shape=jax.ShapeDtypeStruct((HEAD + (n_dp - 1) * largest,), jnp.int32),
        in_specs=[SMEM, SMEM],
        out_specs=SMEM,
        scratch_shapes=[pltpu.SMEM((plane,), jnp.int32)],
    )(place, labels.reshape(-1))

    entry = jnp.arange(n_clus * n_dp * nq, dtype=jnp.int32)
    behind = (row - entry // nq) % n_dp
    order = ((behind * n_clus + entry // (n_dp * nq)) * nq + entry % nq).reshape(1, -1)

    def finish(slots, cap, info, order, first, other, arrived):
        packed = pl.pallas_call(
            functools.partial(owner_kernel, n_dp, cl_own, chips, cap, largest, size),
            out_shape=[shape_of(slots * size, LANES)] * chips,
            in_specs=[SMEM] + [VMEM] * (n_dp - 1),
            out_specs=[VMEM] * chips,
        )(info, *arrived)
        same = [packed[0]] + [in_plane(packed[e], 2 * e) for e in range(1, chips)]
        sibling = [in_plane(s, 1) for s in same]
        blocks = PAIR_CAP * n_dp + 1
        return pl.pallas_call(
            functools.partial(terms_kernel, cl_own, fsplit, chips),
            out_shape=[
                jax.ShapeDtypeStruct((cl_own, width, width), jnp.float32),
                jax.ShapeDtypeStruct((cl_own, width, mq), jnp.float32),
            ],
            in_specs=[SMEM, SMEM] + [VMEM] * (4 + 2 * chips),
            out_specs=[ANY, ANY],
            scratch_shapes=[
                pltpu.VMEM((cl_own, width // LANES, blocks, groups, PIECE, LANES), dtype),
                pltpu.VMEM((cl_own, width, width), jnp.float32),
                pltpu.VMEM((cl_own, width, mq), jnp.float32),
                pltpu.SemaphoreType.DMA((2, cl_own)),
            ],
            compiler_params=pltpu.CompilerParams(vmem_limit_bytes=40 * 2**20),
        )(place, info, query_ids, order, first, other, *same, *sibling)

    most_slots = 2 * PAIR_CAP * (n_dp - 1)
    levels = [c for c in (10, 11, 12, 14) if c < most_slots] + [most_slots]

    def level(slots):
        def run(info, order, first, other, arrived, routes, pieces):
            return tuple(finish(slots, cap, info, order, first, other, arrived))

        return run

    def full_route(info, order, first, other, arrived, routes, pieces):
        arrived = cross_planes(largest, routes, pieces)
        return tuple(finish(most_slots, largest, info, order, first, other, arrived))

    which = jnp.sum((busiest > jnp.array(levels[:-1], jnp.int32)).astype(jnp.int32))
    which = jnp.where(most > cap, len(levels), which)
    branches = [level(c) for c in levels] + [full_route]
    return lax.switch(which, branches, info, order, first, other, arrived, routes, pieces)


def solution(mesh):
    placed = (
        P(AXES, None, None),
        P(AXES, None),
        P(AXES, None),
        P(AXES, None),
    )
    return jax.shard_map(
        local,
        mesh=mesh,
        in_specs=placed,
        out_specs=(P(AXES, None, None), P(AXES, None, None)),
        check_vma=False,
    )
```

```python
import functools

import jax
import jax.numpy as jnp
from jax import lax
from jax.experimental import pallas as pl
from jax.experimental.pallas import tpu as pltpu
from jax.sharding import PartitionSpec as P

MEANROWS = 256
PIECE = 16
LANES = 128
DIGIT = 128
PAIR_CAP = 3
HOP_SLOTS = 12
AXES = ("dp", "clus")
ANY = pl.BlockSpec(memory_space=pl.ANY)
SMEM = pl.BlockSpec(memory_space=pltpu.SMEM)
VMEM = pl.BlockSpec(memory_space=pltpu.VMEM)


def slice_kernel(n_clus, fsplit, labels, points, queries, out, ask):
    nb, _, width = points.shape
    blocks = width // fsplit // LANES
    lane = lax.broadcasted_iota(jnp.int32, (PIECE, LANES), 1)
    tile = jnp.zeros((PIECE, LANES), jnp.float32)
    for b in range(nb):
        label = labels[b]
        tile = jnp.where(lane == 2 * b, (label // DIGIT).astype(jnp.float32), tile)
        tile = jnp.where(lane == 2 * b + 1, lax.rem(label, DIGIT).astype(jnp.float32), tile)
    tile = tile.astype(out.dtype)
    for q in range(n_clus):
        group, part = q // fsplit, q % fsplit
        for b in range(nb):
            for k in range(blocks):
                out[q, pl.ds((b * blocks + k) * PIECE, PIECE), :] = points[
                    b, pl.ds(group * PIECE, PIECE), pl.ds((part * blocks + k) * LANES, LANES)
                ]
        out[q, pl.ds(nb * blocks * PIECE, PIECE), :] = tile
    rows = queries.shape[0]
    for k in range(width // LANES):
        ask[pl.ds(k * rows, rows), :] = queries[:, pl.ds(k * LANES, LANES)]
    ask[pl.ds(width // LANES * rows, PIECE), :] = tile


def quotient(value, by):
    if by & (by - 1):
        return lax.div(value, by)
    return lax.shift_right_logical(value, by.bit_length() - 1)


def remainder(value, by):
    return lax.rem(value, by) if by & (by - 1) else lax.bitwise_and(value, by - 1)


def send_kernel(n_dp, n_clus, nb, cap, routes, pieces, *rest):
    sends, (used,) = rest[: n_dp - 1], rest[n_dp - 1 :]
    size = (pieces.shape[1] - PIECE) // nb
    for hop in range(n_dp):
        used[hop] = 0

    def one(q, carry):
        for b in range(nb):
            hop = quotient(routes[q * nb + b], DIGIT)
            slot = used[hop]
            used[hop] = slot + 1
            at = pl.multiple_of(slot * size, size)
            for d in range(1, n_dp):

                @pl.when((hop == d) & (slot < cap))
                def _():
                    sends[d - 1][pl.ds(at, size), :] = pieces[q, pl.ds(b * size, size), :]

        return carry

    lax.fori_loop(0, n_clus, one, 0)


def own_kernel(n_dp, n_clus, cl_own, nb, routes, pieces, *rest):
    asks, (own, filled) = rest[:n_dp], rest[n_dp:]
    size = (pieces.shape[1] - PIECE) // nb
    for i in range(n_clus * cl_own):
        filled[i] = 0

    def one(q, carry):
        for b in range(nb):
            route = routes[q * nb + b]

            @pl.when(route < DIGIT)
            def _():
                seen = filled[route]
                filled[route] = seen + 1
                slot = jnp.where(remainder(route, cl_own) == 0, seen, PAIR_CAP - 1 - seen)
                at = pl.multiple_of(slot * size, size)
                own[quotient(route, cl_own), pl.ds(at, size), :] = pieces[
                    q, pl.ds(b * size, size), :
                ]

        return carry

    lax.fori_loop(0, n_clus, one, 0)
    length = asks[0].shape[0] - PIECE
    half = length // 2
    sub = lax.broadcasted_iota(jnp.int32, (PIECE, LANES), 0)
    tile = jnp.zeros((PIECE, LANES), jnp.float32)
    for d in range(n_dp):
        tile = jnp.where(sub == d, asks[d][pl.ds(length, PIECE), :].astype(jnp.float32), tile)
    tile = tile.astype(own.dtype)
    base = PAIR_CAP * size
    for q in range(n_clus):
        for d in range(n_dp):
            own[q, pl.ds(base + d * half, half), :] = asks[d][pl.ds(q % 2 * half, half), :]
        own[q, pl.ds(base + n_dp * half, PIECE), :] = tile


def first_kernel(n_dp, n_clus, cl_own, nb, cap, routes, pieces, *rest):
    asks, sends, (own, used, filled) = rest[:n_dp], rest[n_dp : 2 * n_dp - 1], rest[2 * n_dp - 1 :]
    send_kernel(n_dp, n_clus, nb, cap, routes, pieces, *sends, used)
    own_kernel(n_dp, n_clus, cl_own, nb, routes, pieces, *asks, own, filled)


HEAD = 16


def plan_kernel(n_dp, n_clus, cl_own, count, most_sent, place, labels, info, filled):
    row, col = place[0], place[1]
    plane = cl_own * n_clus
    per_chip = 2 * cl_own
    chip = quotient(col, 2)
    for i in range(plane):
        filled[i] = 0

    def tally(i, carry):
        label = labels[count + i]
        inside = remainder(label, plane)
        filled[inside] += (quotient(label, plane) == row).astype(jnp.int32)
        return carry

    lax.fori_loop(0, (n_dp - 1) * count, tally, 0)

    def near(i, seen):
        first = labels[i] - (row * n_clus + col) * cl_own
        return tuple(s + (first == c).astype(jnp.int32) for c, s in enumerate(seen))

    seen = lax.fori_loop(0, count, near, (jnp.int32(0),) * cl_own)
    for c in range(cl_own):
        info[c] = seen[c]
        info[cl_own + c] = filled[col * cl_own + c]
    for first in range(0, plane, per_chip):
        start = jnp.int32(0)
        for i in range(first, first + per_chip):
            held = filled[i]
            filled[i] = start
            start += held
    for c in range(cl_own):
        info[2 * cl_own + c] = filled[col * cl_own + c]

    for hop in range(1, n_dp):

        def one(i, arrived):
            label = labels[hop * count + i]
            mine = quotient(label, plane) == row

            @pl.when(mine)
            def _():
                inside = remainder(label, plane)
                slot = filled[inside]
                filled[inside] = slot + 1
                step = lax.bitwise_xor(quotient(inside, per_chip), chip)
                info[HEAD + (hop - 1) * most_sent + arrived] = step * DIGIT + slot

            return arrived + mine.astype(jnp.int32)

        info[3 * cl_own + hop - 1] = lax.fori_loop(0, count, one, jnp.int32(0))


def owner_kernel(n_dp, cl_own, chips, cap, most_sent, size, info, *rest):
    sources, outs = rest[: n_dp - 1], rest[n_dp - 1 :]
    for hop in range(1, n_dp):

        def one(k, carry):
            code = info[HEAD + (hop - 1) * most_sent + k]
            step, slot = quotient(code, DIGIT), remainder(code, DIGIT)
            at = pl.multiple_of(k * size, size)
            to = pl.multiple_of(slot * size, size)
            for e in range(chips):

                @pl.when(step == e)
                def _():
                    outs[e][pl.ds(to, size), :] = sources[hop - 1][pl.ds(at, size), :]

            return carry

        lax.fori_loop(0, jnp.minimum(info[3 * cl_own + hop - 1], cap), one, 0)


def train_kernel(cl_own, base, place, ids, order, first, other, train):
    entries, width = order.shape[1], train.shape[-1]
    tiles = width // LANES
    core = remainder(place[1], 2)

    def half_table(asked):
        asked = asked.reshape(-1, tiles // 2, PIECE, LANES)
        return jnp.concatenate(
            [asked[:, t].reshape(entries, LANES) for t in range(tiles // 2)], axis=1
        )

    here = half_table(first[:, pl.ds(base, other.shape[1]), :])
    there = half_table(other[...])
    for owned in range(cl_own):
        chosen = jnp.where(order[...] == ids[owned][:, None], 1.0, 0.0).astype(jnp.bfloat16)
        train_here = jnp.dot(chosen, here, preferred_element_type=jnp.float32)
        train_there = jnp.dot(chosen, there, preferred_element_type=jnp.float32)
        train[owned] = jnp.where(
            core == 0,
            jnp.concatenate([train_here, train_there], axis=1),
            jnp.concatenate([train_there, train_here], axis=1),
        ).astype(jnp.bfloat16)


def terms_kernel(cl_own, fsplit, chips, place, info, trains, first, *rest):
    same, sibling, rest = rest[:chips], rest[chips : 2 * chips], rest[2 * chips :]
    gram, cross, rows, gram_acc, cross_acc, out_sems = rest
    tiles = rows.shape[1]
    width = tiles * LANES
    per_part = tiles // fsplit
    size = per_part * PIECE
    n_clus = first.shape[0]
    core = remainder(place[1], 2)

    for owned in range(cl_own):
        near, far = info[owned], info[cl_own + owned]
        total = near + far

        def place_first(k, carry):
            slot = k if owned == 0 else PAIR_CAP - 1 - k
            at = pl.multiple_of(slot * size, size)
            for q in range(n_clus):
                group, part = q // fsplit, q % fsplit
                for t in range(per_part):
                    rows[owned, part * per_part + t, k, group] = first[
                        q, pl.ds(at + t * PIECE, PIECE), :
                    ]
            return carry

        def place_far(k, carry):
            at = pl.multiple_of((info[2 * cl_own + owned] + k) * size, size)
            for e in range(chips):
                for lane, source in enumerate((same[e], sibling[e])):
                    group = 2 * e + lane if fsplit == 1 else e
                    part = 0 if fsplit == 1 else lax.bitwise_xor(core, lane)
                    for t in range(per_part):
                        rows[owned, part * per_part + t, near + k, group] = source[
                            pl.ds(at + t * PIECE, PIECE), :
                        ]
            return carry

        lax.fori_loop(0, near, place_first, 0)
        lax.fori_loop(0, far, place_far, 0)
        for t in range(tiles):
            rows[owned, t, total] = jnp.zeros(rows.shape[3:], rows.dtype)

        train = trains[owned]
        gram_acc[owned] = jnp.zeros(gram_acc.shape[1:], jnp.float32)
        cross_acc[owned] = jnp.zeros(cross_acc.shape[1:], jnp.float32)

        def pair(step, carry):
            block = jnp.concatenate(
                [rows[owned, t, pl.ds(2 * step, 2)].reshape(-1, LANES) for t in range(tiles)],
                axis=1,
            )
            wide = block.astype(jnp.float32)
            squares = jnp.sum(wide * wide, axis=1, keepdims=True)
            weight = lax.rsqrt(squares / width + 1e-06)
            raw = lax.dot_general(
                block, train, (((1,), (1,)), ((), ())), preferred_element_type=jnp.float32
            )
            scores = (raw * weight).astype(jnp.bfloat16)
            over_rows = (((0,), (0,)), ((), ()))
            cross_acc[owned] += (1.0 / MEANROWS) * lax.dot_general(
                block, scores, over_rows, preferred_element_type=jnp.float32
            )
            gram_acc[owned] += (1.0 / MEANROWS) * lax.dot_general(
                block, block, over_rows, preferred_element_type=jnp.float32
            )
            return carry

        lax.fori_loop(0, (total + 1) // 2, pair, 0)
        pltpu.make_async_copy(gram_acc.at[owned], gram.at[owned], out_sems.at[0, owned]).start()
        pltpu.make_async_copy(cross_acc.at[owned], cross.at[owned], out_sems.at[1, owned]).start()
    for owned in range(cl_own):
        pltpu.make_async_copy(gram_acc.at[owned], gram.at[owned], out_sems.at[0, owned]).wait()
        pltpu.make_async_copy(cross_acc.at[owned], cross.at[owned], out_sems.at[1, owned]).wait()


def local(points, block_cluster, queries, query_ids):
    n_clus, n_dp = lax.axis_size("clus"), lax.axis_size("dp")
    nb, blk_rows, width = points.shape
    cl_own, mq = query_ids.shape
    nq = queries.shape[0]
    plane = cl_own * n_clus
    fsplit = max(1, n_clus * PIECE // blk_rows)
    chips = n_clus // 2
    assert cl_own == 2 and nq == PIECE and fsplit <= 2
    assert max(n_clus, n_dp) <= PIECE and plane <= DIGIT and 3 * cl_own + n_dp - 1 <= HEAD
    groups = blk_rows // PIECE
    size = PIECE * width // fsplit // LANES
    length = nq * width // LANES
    count = n_clus * nb
    dtype = points.dtype
    row = lax.axis_index("dp").astype(jnp.int32)
    col = lax.axis_index("clus").astype(jnp.int32)
    place = jnp.stack([row, col])

    def to_plane(sent):
        return lax.all_to_all(sent, "clus", split_axis=0, concat_axis=0, tiled=True)

    def along_dp(sent, hop):
        return lax.ppermute(sent, "dp", [(i, (i + hop) % n_dp) for i in range(n_dp)])

    def in_plane(sent, bits):
        return lax.ppermute(sent, "clus", [(i, i ^ bits) for i in range(n_clus)])

    def read_labels(tile):
        digits = tile[..., : 2 * nb].astype(jnp.int32)
        return digits[..., 0::2] * DIGIT + digits[..., 1::2]

    def shape_of(*dims):
        return jax.ShapeDtypeStruct(dims, dtype)

    sliced, ask = pl.pallas_call(
        functools.partial(slice_kernel, n_clus, fsplit),
        out_shape=[
            shape_of(n_clus, nb * size + PIECE, LANES),
            shape_of(length + PIECE, LANES),
        ],
        in_specs=[SMEM, VMEM, VMEM],
        out_specs=[VMEM, VMEM],
    )(block_cluster[:, 0], points, queries)
    pieces = to_plane(sliced)
    asks = [ask] + [along_dp(ask, d) for d in range(1, n_dp)]

    largest = min(PAIR_CAP * n_clus, count)
    cap = min(HOP_SLOTS * n_clus // 8, largest)
    plane_labels = read_labels(pieces[:, nb * size, :]).reshape(count)
    routes = (plane_labels // plane - row) % n_dp * DIGIT + plane_labels % plane

    def cross_planes(cap, routes, pieces):
        sends = pl.pallas_call(
            functools.partial(send_kernel, n_dp, n_clus, nb, cap),
            out_shape=[shape_of(cap * size, LANES)] * (n_dp - 1),
            in_specs=[SMEM, VMEM],
            out_specs=[VMEM] * (n_dp - 1),
            scratch_shapes=[pltpu.SMEM((n_dp,), jnp.int32)],
        )(routes, pieces)
        return [along_dp(sends[d - 1], d) for d in range(1, n_dp)]

    *sends, own = pl.pallas_call(
        functools.partial(first_kernel, n_dp, n_clus, cl_own, nb, cap),
        out_shape=[shape_of(cap * size, LANES)] * (n_dp - 1)
        + [shape_of(n_clus, PAIR_CAP * size + n_dp * length // 2 + PIECE, LANES)],
        in_specs=[SMEM] + [VMEM] * (1 + n_dp),
        out_specs=[VMEM] * n_dp,
        scratch_shapes=[pltpu.SMEM((n_dp,), jnp.int32), pltpu.SMEM((plane,), jnp.int32)],
    )(routes, pieces, *asks)
    arrived = [along_dp(sends[d - 1], d) for d in range(1, n_dp)]
    first = to_plane(own)
    base = PAIR_CAP * size
    other = in_plane(first[:, base : base + n_dp * length // 2], 1)

    labels = read_labels(first[:, base + n_dp * length // 2 :][:, :n_dp])
    labels = labels.transpose(1, 0, 2).reshape(n_dp, count)
    hop = lax.broadcasted_iota(jnp.int32, (n_dp, count), 0)
    hops_to_go = (labels // plane - row + hop) % n_dp
    pair_of = jnp.where(hops_to_go > 0, hop * n_dp + hops_to_go, -1).reshape(1, -1)
    pairs = lax.broadcasted_iota(jnp.int32, (n_dp * n_dp, 1), 0)
    most = jnp.max(jnp.sum((pair_of == pairs).astype(jnp.int32), axis=1))
    chip_of = jnp.where(hops_to_go > 0, labels // (2 * cl_own), -1).reshape(1, -1)
    all_chips = lax.broadcasted_iota(jnp.int32, (n_dp * chips, 1), 0)
    busiest = jnp.max(jnp.sum((chip_of == all_chips).astype(jnp.int32), axis=1))

    info = pl.pallas_call(
        functools.partial(plan_kernel, n_dp, n_clus, cl_own, count, largest),
        out_shape=jax.ShapeDtypeStruct((HEAD + (n_dp - 1) * largest,), jnp.int32),
        in_specs=[SMEM, SMEM],
        out_specs=SMEM,
        scratch_shapes=[pltpu.SMEM((plane,), jnp.int32)],
    )(place, labels.reshape(-1))

    entry = jnp.arange(n_clus * n_dp * nq, dtype=jnp.int32)
    behind = (row - entry // nq) % n_dp
    order = ((behind * n_clus + entry // (n_dp * nq)) * nq + entry % nq).reshape(1, -1)

    train = pl.pallas_call(
        functools.partial(train_kernel, cl_own, base),
        out_shape=shape_of(cl_own, mq, width),
        in_specs=[SMEM] + [VMEM] * 4,
        out_specs=VMEM,
    )(place, query_ids, order, first, other)

    def finish(slots, cap, info, train, first, arrived):
        packed = pl.pallas_call(
            functools.partial(owner_kernel, n_dp, cl_own, chips, cap, largest, size),
            out_shape=[shape_of(slots * size, LANES)] * chips,
            in_specs=[SMEM] + [VMEM] * (n_dp - 1),
            out_specs=[VMEM] * chips,
        )(info, *arrived)
        same = [packed[0]] + [in_plane(packed[e], 2 * e) for e in range(1, chips)]
        sibling = [in_plane(s, 1) for s in same]
        blocks = PAIR_CAP * n_dp + 1
        return pl.pallas_call(
            functools.partial(terms_kernel, cl_own, fsplit, chips),
            out_shape=[
                jax.ShapeDtypeStruct((cl_own, width, width), jnp.float32),
                jax.ShapeDtypeStruct((cl_own, width, mq), jnp.float32),
            ],
            in_specs=[SMEM, SMEM] + [VMEM] * (2 + 2 * chips),
            out_specs=[ANY, ANY],
            scratch_shapes=[
                pltpu.VMEM((cl_own, width // LANES, blocks, groups, PIECE, LANES), dtype),
                pltpu.VMEM((cl_own, width, width), jnp.float32),
                pltpu.VMEM((cl_own, width, mq), jnp.float32),
                pltpu.SemaphoreType.DMA((2, cl_own)),
            ],
            compiler_params=pltpu.CompilerParams(vmem_limit_bytes=40 * 2**20),
        )(place, info, train, first, *same, *sibling)

    most_slots = 2 * PAIR_CAP * (n_dp - 1)
    levels = [c for c in (9, 10, 11, 12, 14) if c < most_slots] + [most_slots]

    def level(slots):
        def run(info, train, first, arrived, routes, pieces):
            return tuple(finish(slots, cap, info, train, first, arrived))

        return run

    def full_route(info, train, first, arrived, routes, pieces):
        arrived = cross_planes(largest, routes, pieces)
        return tuple(finish(most_slots, largest, info, train, first, arrived))

    which = jnp.sum((busiest > jnp.array(levels[:-1], jnp.int32)).astype(jnp.int32))
    which = jnp.where(most > cap, len(levels), which)
    branches = [level(c) for c in levels] + [full_route]
    return lax.switch(which, branches, info, train, first, arrived, routes, pieces)


def solution(mesh):
    placed = (
        P(AXES, None, None),
        P(AXES, None),
        P(AXES, None),
        P(AXES, None),
    )
    return jax.shard_map(
        local,
        mesh=mesh,
        in_specs=placed,
        out_specs=(P(AXES, None, None), P(AXES, None, None)),
        check_vma=False,
    )
```
